128 devices in a mesh: gx: 8 (over x, core), gy: 16 (over z, y).
Axes of the slice: x: 4, y: 4, z: 4, core: 2. Of those that a mesh axis runs over, the one named last changes fastest.
Arguments:
- multipliers: bfloat16 [8, 16, 256, 2, 640], P('gx', 'gy'), may hold values from -6 to 6
- partner: int32 [8, 16, 2, 640], P('gx', 'gy'), may hold values from 0 to 639, each once within a row
- interface_rows: int32 [8, 16, 2608], P('gx', 'gy'), may hold values from 0 to 3071, as said below
- block_mask: int32 [8, 16, 16, 16], P('gx', 'gy'), may hold values 0 or 1
- tiles: bfloat16 [8, 16, 3072, 3072], P('gx', 'gy')
- basis: bfloat16 [8, 16, 48, 3072], P('gx', 'gy'), may hold values from -1.1953125 to 1.1953125
- coarse_inverse: bfloat16 [1536, 1536], replicated, may hold values from -0.15625 to 0.15625
Outputs:
- jumps: bfloat16 [8, 16, 256, 2, 640], P('gx', 'gy')
- curvature: float32 [256], replicated
The draws below stay inside these ranges and needn't reach their ends.
Inputs may be any that keep to these rules, and one draw needn't show every extreme that they name: `interface_rows`: each subdomain's rows are distinct.
All inputs are finite; a program needn't handle non-finite values. No bound on the sum of `block_mask` on one device may be relied on, other than what follows from the above.
Results may differ from the reference program's by a relative error of at most 0.006.
Values may be sent and summed in bfloat16 or wider, within the bound.
A program may use at most 192 MiB of HBM per device.

```python
import jax
import jax.numpy as jnp
from jax import lax

NI = 3072
BS = 192
F = 640
CD = 12
R = 256
NB = 16
NC = 1536
N_GX = 8
N_GY = 16


def draw_interface_rows(key, part):
    key = jax.random.fold_in(key, 11)
    keys = jax.random.split(key, N_GX * N_GY)
    perms = jax.vmap(lambda k: jax.random.permutation(k, NI))(keys)[:, :4 * F + 4 * CD]
    return perms.reshape(N_GX, N_GY, 4 * F + 4 * CD).astype(jnp.int32)


def draw_tiles(key, part):
    key = jax.random.fold_in(key, 23)
    shape = (N_GX, N_GY, NI, NI)
    noise = jax.random.normal(key, shape, jnp.float32)
    rows = lax_iota(NI)
    diag = (rows[:, None] == rows[None, :]).astype(jnp.float32)
    return (noise * NI ** (-0.5) + 1.5 * diag).astype(jnp.bfloat16)


def lax_iota(count):
    return jnp.arange(count, dtype=jnp.int32)


def with_ends(values, own_key, least, high):
    index_at = [jax.random.randint(jax.random.fold_in(own_key, axis), (), 0, length) for axis, length in enumerate(values.shape)]
    longest = values.shape.index(max(values.shape))
    beside = index_at[:longest] + [(index_at[longest] + 1) % values.shape[longest]] + index_at[longest + 1:]
    return values.at[tuple(index_at)].set(least).at[tuple(beside)].set(high)


def shard_levels(key, shape, cuts, least, largest):
    factor_of = 1.0
    for dim, blocks in cuts:
        heights = jax.random.uniform(jax.random.fold_in(jax.random.fold_in(key, 6), dim), (blocks,), jnp.float32, least / len(cuts), largest / len(cuts))
        factor_of = factor_of * jnp.repeat(jnp.exp(heights), shape[dim] // blocks).reshape((-1,) + (1,) * (len(shape) - 1 - dim))
    return factor_of


def scatter_about(own_key, extent, width, most, cuts=(), kind=jnp.bfloat16):
    entries = jax.random.normal(own_key, extent, jnp.float32) * width
    if len(cuts) > 0:
        entries = shard_levels(own_key, extent, cuts, -0.22, 0.18) * entries
    return jnp.clip(entries, min=-most, max=most).astype(kind)


def setup_inputs(seed: int = 0) -> dict:
    key_list = jax.random.split(jax.random.key(seed), 8)
    return {
        "multipliers": scatter_about(key_list[0], (N_GX, N_GY, R, 2, F), 1.0, 6.0, ((0, 8), (1, 16))),
        "partner": jax.vmap(lambda own: jax.random.permutation(own, F))(jax.random.split(key_list[1], N_GX * N_GY * 2)).reshape((N_GX, N_GY, 2, F)).astype(jnp.int32),
        "interface_rows": draw_interface_rows(jax.random.fold_in(key_list[7], 71), 0),
        "block_mask": with_ends((jax.random.randint(key_list[3], (N_GX, N_GY, NB, NB), 0, 5) < 3).astype(jnp.int32), jax.random.fold_in(key_list[3], 1), 0, 1),
        "tiles": draw_tiles(jax.random.fold_in(key_list[7], 71), 0),
        "basis": scatter_about(key_list[5], (N_GX, N_GY, 4 * CD, NI), 0.2, 1.1953125, ((0, 8), (1, 16))),
        "coarse_inverse": scatter_about(key_list[6], (NC, NC), NC ** -0.5, 0.15625),
    }


def place(values, perm):
    return jnp.zeros_like(values).at[:, perm].set(values)


def reference(multipliers, partner, interface_rows, block_mask, tiles, basis, coarse_inverse):
    east_lam = multipliers[:, :, :, 0, :]
    south_lam = multipliers[:, :, :, 1, :]
    placed_east = jax.vmap(jax.vmap(place))(east_lam, partner[:, :, 0, :])
    placed_south = jax.vmap(jax.vmap(place))(south_lam, partner[:, :, 1, :])
    from_west = jnp.roll(placed_east, 1, axis=1)
    from_north = jnp.roll(placed_south, 1, axis=0)
    count = N_GX * N_GY
    flat_rows = interface_rows.reshape(count, 4 * F + 4 * CD)

    def spread_one(args):
        rows, lam_e, lam_s, in_w, in_n = args
        spread = jnp.zeros((R, NI), jnp.bfloat16)
        spread = spread.at[:, rows[3 * F:4 * F]].set(lam_e)
        spread = spread.at[:, rows[F:2 * F]].set(lam_s)
        spread = spread.at[:, rows[2 * F:3 * F]].set(-in_w)
        spread = spread.at[:, rows[0:F]].set(-in_n)
        return spread

    spreads = lax.map(spread_one, (flat_rows, east_lam.reshape(count, R, F), south_lam.reshape(count, R, F), from_west.reshape(count, R, F), from_north.reshape(count, R, F)))

    def image_one(args):
        spread, tile, mask, rows = args
        masked = (tile.reshape(NB, BS, NB, BS) * mask.astype(jnp.bfloat16)[:, None, :, None]).reshape(NI, NI)
        local = jnp.dot(spread, masked, preferred_element_type=jnp.float32)
        return local, local[:, rows[4 * F:]]

    local_image, corner_load = lax.map(image_one, (spreads, tiles.reshape(count, NI, NI), block_mask.reshape(count, NB, NB), flat_rows))
    cv = corner_load.reshape(N_GX, N_GY, R, 4, CD)
    grid = cv[:, :, :, 0] + jnp.roll(cv[:, :, :, 1], 1, axis=1) + jnp.roll(cv[:, :, :, 2], 1, axis=0) + jnp.roll(jnp.roll(cv[:, :, :, 3], 1, axis=0), 1, axis=1)
    coarse_load = jnp.transpose(grid, (2, 0, 1, 3)).reshape(R, NC).astype(jnp.bfloat16)
    coarse_solution = jnp.dot(coarse_load, coarse_inverse, preferred_element_type=jnp.float32)
    zg = jnp.transpose(coarse_solution.reshape(R, N_GX, N_GY, CD), (1, 2, 0, 3))
    corner_values = jnp.stack([zg, jnp.roll(zg, -1, axis=1), jnp.roll(zg, -1, axis=0), jnp.roll(jnp.roll(zg, -1, axis=0), -1, axis=1)], axis=3)
    corner_values = corner_values.reshape(count, R, 4 * CD).astype(jnp.bfloat16)

    def finish_one(args):
        local, corners, phi, rows, spread = args
        image = local - jnp.dot(corners, phi, preferred_element_type=jnp.float32)
        faces = image[:, rows[:4 * F]].astype(jnp.bfloat16).reshape(R, 4, F)
        product = jnp.sum(spread.astype(jnp.float32) * image, axis=1)
        return faces, product

    face_values, products = lax.map(finish_one, (local_image, corner_values, basis.reshape(count, 4 * CD, NI), flat_rows, spreads))
    face_values = face_values.reshape(N_GX, N_GY, R, 4, F)
    east_nbr_west = jnp.roll(face_values[:, :, :, 2], -1, axis=1)
    south_nbr_north = jnp.roll(face_values[:, :, :, 0], -1, axis=0)
    take = jax.vmap(jax.vmap(lambda vals, perm: jnp.take(vals, perm, axis=1)))
    jump_e = face_values[:, :, :, 3].astype(jnp.float32) - take(east_nbr_west, partner[:, :, 0, :]).astype(jnp.float32)
    jump_s = face_values[:, :, :, 1].astype(jnp.float32) - take(south_nbr_north, partner[:, :, 1, :]).astype(jnp.float32)
    jumps = jnp.stack([jump_e, jump_s], axis=3).astype(jnp.bfloat16)
    curvature = jnp.sum(products, axis=0) / (2.0 * F * N_GX * N_GY)
    return jumps, curvature
```

```python
import functools

import jax
import jax.numpy as jnp
from jax import lax
from jax.experimental import pallas as pl
from jax.experimental.pallas import tpu as pltpu
from jax.sharding import PartitionSpec as P

MESH = pl.DeviceIdType.MESH
BF16 = jnp.bfloat16
F32 = jnp.float32
I32 = jnp.int32
NT = (((1,), (1,)), ((), ()))


def dot(x, y):
    return jnp.dot(x, y, preferred_element_type=F32)


def dot_nt(x, y):
    return lax.dot_general(x, y, NT, preferred_element_type=F32)


def iota(shape, dim):
    return lax.broadcasted_iota(I32, shape, dim)


def unit(cond):
    return jnp.where(cond, jnp.ones((), BF16), jnp.zeros((), BF16))


def one_hot(first, count, index):
    rows = iota((count, index.shape[1]), 0).astype(jnp.int16)
    return unit(rows == (index - first).astype(jnp.int16))


def kernel(
    nx,
    ny,
    lam_hbm,
    partner_hbm,
    rows_hbm,
    mask_hbm,
    tile_hbm,
    basis_hbm,
    inverse_hbm,
    jumps_ref,
    curvature_ref,
    lam,
    partner,
    rows,
    mask,
    tile,
    basis,
    inverse,
    own,
    received,
    partner_west,
    partner_north,
    index,
    spread,
    local,
    image,
    mask_rows,
    corner_tile,
    solve,
    loads,
    parts,
    parts_in,
    face_out,
    face_in,
    face_own,
    sum_x,
    sum_y,
    local_sem,
    pair_send,
    pair_recv,
    load_send,
    load_recv,
    part_send,
    part_recv,
    sumx_send,
    sumx_recv,
    sumy_send,
    sumy_recv,
):
    a = lax.axis_index("gx")
    b = lax.axis_index("gy")
    nrhs, _, faces = lam.shape
    width = tile.shape[0]
    nblock = mask.shape[0]
    bsize = width // nblock
    group = bsize // 16
    four_cd = basis.shape[0]
    cd = four_cd // 4
    row_cd = ny * cd
    two = 2 * faces
    chunks = 4
    tall = width // chunks
    blocks = nblock // chunks
    wide = width // 3
    east = (a, lax.rem(b + 1, ny))
    west = (a, lax.rem(b + ny - 1, ny))
    south = (lax.rem(a + 1, nx), b)
    north = (lax.rem(a + nx - 1, nx), b)

    def fetch(src, dst, slot):
        copy = pltpu.make_async_copy(src, dst, local_sem.at[slot])
        copy.start()
        return copy

    lam_copy = fetch(lam_hbm, lam, 0)
    rows_copy = fetch(rows_hbm, rows, 1)
    partner_copy = fetch(partner_hbm, partner, 2)
    mask_copy = fetch(mask_hbm, mask, 3)

    def tile_copy(j):
        part = pl.ds(pl.multiple_of(j * tall, tall), tall)
        return pltpu.make_async_copy(tile_hbm.at[part], tile.at[part], local_sem.at[8 + j])

    barrier = pltpu.get_barrier_semaphore()

    @pl.loop(1, ny)
    def _(k):
        pl.semaphore_signal(barrier, inc=1, device_id=(a, lax.rem(b + k, ny)), device_id_type=MESH)

    @pl.loop(1, nx)
    def _(k):
        pl.semaphore_signal(barrier, inc=1, device_id=(lax.rem(a + k, nx), b), device_id_type=MESH)

    for j in range(chunks):
        tile_copy(j).start()
    basis_copy = fetch(basis_hbm, basis, 4)
    inverse_copies = []
    for p in range(2):
        first = pl.multiple_of(lax.rem(a + p, nx) * row_cd, 16)
        inverse_copies.append(
            fetch(inverse_hbm.at[pl.ds(first, row_cd)], inverse.at[pl.ds(p * row_cd, row_cd)], 5 + p)
        )

    lam_copy.wait()
    both = lam[...].reshape(2 * nrhs, faces)
    for f in range(2):
        pick = unit(iota((nrhs, 2 * nrhs), 1) == 2 * iota((nrhs, 2 * nrhs), 0) + f)
        own[:, f * faces : (f + 1) * faces] = dot(pick, both).astype(BF16)
    partner_copy.wait()
    pl.semaphore_wait(barrier, nx + ny - 2)

    def send(src, dst, slot, device):
        copy = pltpu.make_async_remote_copy(
            src_ref=src,
            dst_ref=dst,
            send_sem=pair_send.at[slot],
            recv_sem=pair_recv.at[slot],
            device_id=device,
            device_id_type=MESH,
        )
        copy.start()
        return copy

    east_half = pl.ds(0, faces)
    south_half = pl.ds(faces, faces)
    pairs = [
        send(partner, partner_west, 0, east),
        send(partner, partner_north, 1, south),
        send(own.at[:, east_half], received.at[:, east_half], 2, east),
        send(own.at[:, south_half], received.at[:, south_half], 3, south),
    ]

    rows_copy.wait()
    index[:, 0:faces] = rows[:, 3 * faces : 4 * faces]
    index[:, faces:two] = rows[:, faces:two]

    @pl.loop(0, 3)
    def _(j):
        n0 = pl.multiple_of(j * wide, wide)
        hot = one_hot(n0, wide, index[:, 0:two])
        spread[:, pl.ds(n0, wide)] = dot_nt(own[...], hot).astype(BF16)

    mask_copy.wait()
    inside = iota((nblock, width), 1) - bsize * iota((nblock, width), 0)
    expanded = dot(
        mask[...].astype(F32).astype(BF16), unit((inside >= 0) & (inside < bsize))
    )
    for i in range(nblock):
        mask_rows[i] = jnp.broadcast_to(expanded[i : i + 1], (16, width)).astype(BF16)

    corner_rows = rows[:, 4 * faces : 4 * faces + four_cd]
    corner_hot = one_hot(0, width, corner_rows)

    @pl.loop(0, chunks)
    def _(j):
        tile_copy(j).wait()
        part = pl.ds(pl.multiple_of(j * tall, tall), tall)
        piece = tile[part].reshape(blocks, group, 16, width)
        piece = piece * mask_rows[pl.ds(j * blocks, blocks)][:, None]
        corner_tile[part] = dot(piece.reshape(tall, width), corner_hot).astype(BF16)

    for copy in inverse_copies:
        copy.wait()
    total = inverse.shape[1]

    def over(value, count):
        return jnp.where(value >= count, value - count, value)

    def divided(value):
        return (value * (-(-(1 << 19) // cd))) >> 19

    out = iota((nx * four_cd, 1), 0)
    unit_at = divided(out)
    corner = unit_at & 3
    node = over((unit_at >> 2) + (corner >> 1), nx) * ny + over(b + (corner & 1), ny)
    column = node * cd + out - unit_at * cd
    chosen = unit(iota((nx * four_cd, total), 1) == column)
    by_row = dot_nt(chosen, inverse[...]).astype(BF16)
    load_at = iota((1, ny * four_cd), 1)
    unit_at = divided(load_at)
    corner = unit_at & 3
    source = (corner >> 1) * row_cd + over((unit_at >> 2) + (corner & 1), ny) * cd
    source = source + load_at - unit_at * cd
    widen = unit(iota((2 * row_cd, ny * four_cd), 0) == source)
    solve[...] = dot(by_row, widen).astype(BF16)

    for f, copy in enumerate(pairs[:2]):
        copy.wait()
        pair_row = (partner_west[0:1], partner_north[1:2])[f]
        face_row = (rows[:, two : 3 * faces], rows[:, 0:faces])[f]
        sub = iota((8, faces), 0)
        digits = jnp.where(sub == 0, face_row >> 8, jnp.where(sub == 1, face_row & 255, 0))
        found = dot(digits.astype(F32).astype(BF16), one_hot(0, faces, pair_row))
        index[:, two + f * faces : two + (f + 1) * faces] = (
            found[0:1] * 256.0 + found[1:2]
        ).astype(I32)
    pairs[3].wait()
    pairs[2].wait()

    @pl.loop(0, 3)
    def _(j):
        n0 = pl.multiple_of(j * wide, wide)
        hot = one_hot(n0, wide, index[:, two : 2 * two])
        at = (slice(None), pl.ds(n0, wide))
        spread[at] = (spread[at].astype(F32) - dot_nt(received[...], hot)).astype(BF16)

    corner_load = dot(spread[...], corner_tile[...]).astype(BF16)
    same = unit(iota((four_cd, four_cd), 0) == iota((four_cd, four_cd), 1))
    mine = pl.ds(pl.multiple_of(b * four_cd, 16), four_cd)
    loads[mine] = dot_nt(same, corner_load).astype(BF16)

    def load_copy(k):
        return pltpu.make_async_remote_copy(
            src_ref=loads.at[mine],
            dst_ref=loads.at[mine],
            send_sem=load_send.at[k],
            recv_sem=load_recv.at[k],
            device_id=(a, lax.rem(b + k, ny)),
            device_id_type=MESH,
        )

    pl.loop(1, ny)(lambda k: load_copy(k).start())

    @pl.loop(0, 3)
    def _(j):
        at = (slice(None), pl.ds(pl.multiple_of(j * wide, wide), wide))
        masked = tile[at].reshape(nblock, group, 16, wide) * mask_rows[:, :, at[1]][:, None]
        local[at] = dot(spread[...], masked.reshape(width, wide))

    pl.loop(1, ny)(lambda k: load_copy(k).wait())

    parts[...] = dot(solve[...], loads[...]).astype(BF16)

    def part_copy(k):
        to = lax.rem(a + k, nx)
        return pltpu.make_async_remote_copy(
            src_ref=parts.at[pl.ds(pl.multiple_of(to * four_cd, 16), four_cd)],
            dst_ref=parts_in.at[k],
            send_sem=part_send.at[k],
            recv_sem=part_recv.at[k],
            device_id=(to, b),
            device_id_type=MESH,
        )

    pl.loop(1, nx)(lambda k: part_copy(k).start())
    basis_copy.wait()
    corners = parts[pl.ds(pl.multiple_of(a * four_cd, 16), four_cd)].astype(F32)
    for k in range(1, nx):
        part_copy(k).wait()
        corners = corners + parts_in[k].astype(F32)
    corners = corners.T.astype(BF16)

    product = jnp.zeros((nrhs, 128), F32)
    for j in range(3):
        at = (slice(None), slice(j * wide, (j + 1) * wide))
        full = local[at] - dot(corners, basis[at])
        image[at] = full.astype(BF16)
        full = full * spread[at].astype(F32)
        for q in range(wide // 128):
            product = product + full[:, q * 128 : (q + 1) * 128]
    mine_x = pl.ds(pl.multiple_of(a * 8, 8), 8)
    sum_x[mine_x] = lax.dot_general(
        jnp.ones((8, 128), F32), product, NT, precision=lax.Precision.HIGHEST, preferred_element_type=F32
    )

    def sumx_copy(k):
        return pltpu.make_async_remote_copy(
            src_ref=sum_x.at[mine_x],
            dst_ref=sum_x.at[mine_x],
            send_sem=sumx_send.at[k],
            recv_sem=sumx_recv.at[k],
            device_id=(lax.rem(a + k, nx), b),
            device_id_type=MESH,
        )

    pl.loop(1, nx)(lambda k: sumx_copy(k).start())

    def gathered(first, count):
        return dot(image[...], one_hot(0, width, index[:, first : first + count])).astype(BF16)

    face_out[:, 0:faces] = gathered(two, faces)
    pairs.append(send(face_out.at[:, east_half], face_in.at[:, east_half], 4, west))
    face_out[:, faces:two] = gathered(two + faces, faces)
    pairs.append(send(face_out.at[:, south_half], face_in.at[:, south_half], 5, north))

    pl.loop(1, nx)(lambda k: sumx_copy(k).wait())
    mine_y = pl.ds(pl.multiple_of(b * 8, 8), 8)
    sum_y[mine_y] = jnp.sum(sum_x[...].reshape(nx, 8, nrhs), axis=0)

    def sumy_copy(k):
        return pltpu.make_async_remote_copy(
            src_ref=sum_y.at[mine_y],
            dst_ref=sum_y.at[mine_y],
            send_sem=sumy_send.at[k],
            recv_sem=sumy_recv.at[k],
            device_id=(a, lax.rem(b + k, ny)),
            device_id_type=MESH,
        )

    pl.loop(1, ny)(lambda k: sumy_copy(k).start())
    face_own[...] = gathered(0, two)
    pl.loop(1, ny)(lambda k: sumy_copy(k).wait())
    everything = jnp.sum(sum_y[...].reshape(ny, 8, nrhs), axis=0)
    curvature_ref[...] = everything[0:1] / (2.0 * faces * nx * ny)

    pairs[5].wait()
    pairs[4].wait()
    jump = (face_own[...].astype(F32) - face_in[...].astype(F32)).astype(BF16)
    mixed = jnp.zeros((2 * nrhs, faces), F32)
    for f in range(2):
        lay = unit(iota((2 * nrhs, nrhs), 0) == 2 * iota((2 * nrhs, nrhs), 1) + f)
        mixed = mixed + dot(lay, jump[:, f * faces : (f + 1) * faces])
    jumps_ref[...] = mixed.astype(BF16).reshape(nrhs, 2, faces)


def shards(multipliers, partner, interface_rows, block_mask, tiles, basis, coarse_inverse):
    nx = lax.axis_size("gx")
    ny = lax.axis_size("gy")
    lam = multipliers[0, 0]
    nrhs, _, faces = lam.shape
    rows = interface_rows[0]
    width = tiles.shape[2]
    nblock = block_mask.shape[2]
    four_cd = basis.shape[2]
    total = coarse_inverse.shape[1]
    row_cd = total // nx
    dma = pltpu.SemaphoreType.DMA
    vmem = pltpu.VMEM
    two = 2 * faces
    jumps, curvature = pl.pallas_call(
        functools.partial(kernel, nx, ny),
        out_shape=(
            jax.ShapeDtypeStruct(lam.shape, BF16),
            jax.ShapeDtypeStruct((1, nrhs), F32),
        ),
        in_specs=[pl.BlockSpec(memory_space=pl.ANY)] * 7,
        out_specs=(pl.BlockSpec(memory_space=vmem), pl.BlockSpec(memory_space=vmem)),
        scratch_shapes=[
            vmem(lam.shape, BF16),
            vmem((2, faces), I32),
            vmem(rows.shape, I32),
            vmem((nblock, nblock), I32),
            vmem((width, width), BF16),
            vmem((four_cd, width), BF16),
            vmem((2 * row_cd, total), BF16),
            vmem((nrhs, two), BF16),
            vmem((nrhs, two), BF16),
            vmem((2, faces), I32),
            vmem((2, faces), I32),
            vmem((1, 2 * two), I32),
            vmem((nrhs, width), BF16),
            vmem((nrhs, width), F32),
            vmem((nrhs, width), BF16),
            vmem((nblock, 16, width), BF16),
            vmem((width, four_cd), BF16),
            vmem((nx * four_cd, ny * four_cd), BF16),
            vmem((ny * four_cd, nrhs), BF16),
            vmem((nx * four_cd, nrhs), BF16),
            vmem((nx, four_cd, nrhs), BF16),
            vmem((nrhs, two), BF16),
            vmem((nrhs, two), BF16),
            vmem((nrhs, two), BF16),
            vmem((nx * 8, nrhs), F32),
            vmem((ny * 8, nrhs), F32),
            dma((12,)),
            dma((6,)),
            dma((6,)),
            dma((ny,)),
            dma((ny,)),
            dma((nx,)),
            dma((nx,)),
            dma((nx,)),
            dma((nx,)),
            dma((ny,)),
            dma((ny,)),
        ],
        compiler_params=pltpu.CompilerParams(
            collective_id=0, has_side_effects=True, vmem_limit_bytes=60 * 2**20
        ),
    )(lam, partner[0, 0], rows, block_mask[0, 0], tiles[0, 0], basis[0, 0], coarse_inverse)
    return jumps[None, None], curvature.reshape(nrhs)


def solution(mesh):
    in_specs = (
        P("gx", "gy", None, None, None),
        P("gx", "gy", None, None),
        P("gx", "gy", None),
        P("gx", "gy", None, None),
        P("gx", "gy", None, None),
        P("gx", "gy", None, None),
        P(),
    )
    out_specs = (P("gx", "gy", None, None, None), P())
    return jax.shard_map(shards, mesh=mesh, in_specs=in_specs, out_specs=out_specs, check_vma=False)
```

```python
import functools

import jax
import jax.numpy as jnp
from jax import lax
from jax.experimental import pallas as pl
from jax.experimental.pallas import tpu as pltpu
from jax.sharding import PartitionSpec as P

MESH = pl.DeviceIdType.MESH
BF16 = jnp.bfloat16
F32 = jnp.float32
I32 = jnp.int32
NT = (((1,), (1,)), ((), ()))


def dot(x, y):
    return jnp.dot(x, y, preferred_element_type=F32)


def dot_nt(x, y):
    return lax.dot_general(x, y, NT, preferred_element_type=F32)


def iota(shape, dim):
    return lax.broadcasted_iota(I32, shape, dim)


def unit(cond):
    return jnp.where(cond, jnp.ones((), BF16), jnp.zeros((), BF16))


def one_hot(first, count, index):
    rows = iota((count, index.shape[1]), 0).astype(jnp.int16)
    return unit(rows == (index - first).astype(jnp.int16))


def kernel(
    nx,
    ny,
    lam_hbm,
    partner_hbm,
    rows_hbm,
    mask_hbm,
    tile_hbm,
    basis_hbm,
    inverse_hbm,
    jump_ref,
    curvature_ref,
    lam,
    partner,
    rows,
    mask,
    tile,
    joint,
    inverse,
    own,
    received,
    partner_west,
    partner_north,
    index,
    spread,
    product,
    image,
    mask_rows,
    solve,
    loads,
    bilinear,
    stack,
    basis_out,
    parts,
    parts_in,
    face_out,
    face_in,
    face_own,
    sum_x,
    sum_y,
    local_sem,
    pair_send,
    pair_recv,
    load_send,
    load_recv,
    bil_send,
    bil_recv,
    part_send,
    part_recv,
    sumx_send,
    sumx_recv,
    sumy_send,
    sumy_recv,
):
    a = lax.axis_index("gx")
    b = lax.axis_index("gy")
    nrhs, _, faces = lam.shape
    width = tile.shape[0]
    nblock = mask.shape[0]
    bsize = width // nblock
    group = bsize // 16
    four_cd = basis_hbm.shape[0]
    cd = four_cd // 4
    row_cd = ny * cd
    two = 2 * faces
    chunks = 4
    tall = width // chunks
    blocks = nblock // chunks
    wide = width // 3
    east = (a, lax.rem(b + 1, ny))
    west = (a, lax.rem(b + ny - 1, ny))
    south = (lax.rem(a + 1, nx), b)
    north = (lax.rem(a + nx - 1, nx), b)

    def fetch(src, dst, slot):
        copy = pltpu.make_async_copy(src, dst, local_sem.at[slot])
        copy.start()
        return copy

    half = nrhs // 2
    lam_copies = [
        fetch(lam_hbm.at[pl.ds(h * half, half)], lam.at[pl.ds(h * half, half)], (0, 7)[h]) for h in range(2)
    ]
    rows_copy = fetch(rows_hbm, rows, 1)
    partner_copy = fetch(partner_hbm, partner, 2)
    mask_copy = fetch(mask_hbm, mask, 3)

    def tile_copy(j):
        part = pl.ds(pl.multiple_of(j * tall, tall), tall)
        return pltpu.make_async_copy(tile_hbm.at[part], tile.at[part], local_sem.at[8 + j])

    barrier = pltpu.get_barrier_semaphore()

    @pl.loop(1, ny)
    def _(k):
        pl.semaphore_signal(barrier, inc=1, device_id=(a, lax.rem(b + k, ny)), device_id_type=MESH)

    @pl.loop(1, nx)
    def _(k):
        pl.semaphore_signal(barrier, inc=1, device_id=(lax.rem(a + k, nx), b), device_id_type=MESH)

    for j in range(chunks):
        tile_copy(j).start()
    basis_rows = pl.ds(nrhs, four_cd)
    basis_copies = [
        fetch(basis_hbm, joint.at[pl.ds(four_cd, four_cd)], 4),
        fetch(basis_hbm, image.at[basis_rows], 12),
    ]
    inverse_copies = []
    for p in range(2):
        first = pl.multiple_of(lax.rem(a + p, nx) * row_cd, 16)
        inverse_copies.append(
            fetch(inverse_hbm.at[pl.ds(first, row_cd)], inverse.at[pl.ds(p * row_cd, row_cd)], 5 + p)
        )

    def send(src, dst, slot, device):
        copy = pltpu.make_async_remote_copy(
            src_ref=src,
            dst_ref=dst,
            send_sem=pair_send.at[slot],
            recv_sem=pair_recv.at[slot],
            device_id=device,
            device_id_type=MESH,
        )
        copy.start()
        return copy

    east_half = pl.ds(0, faces)
    south_half = pl.ds(faces, faces)
    at_row, at_column = iota((nrhs, nrhs), 0), iota((nrhs, nrhs), 1)
    pick = unit(at_column == jnp.where(at_row < half, 2 * at_row, 2 * (at_row - half) + 1))
    pairs = []
    for h in range(2):
        part = pl.ds(h * half, half)
        lam_copies[h].wait()
        apart = dot(pick, lam[part].reshape(nrhs, faces)).astype(BF16)
        own[part, 0:faces] = apart[:half]
        own[part, faces:two] = apart[half:]
        if h == 0:
            partner_copy.wait()
            pl.semaphore_wait(barrier, nx + ny - 2)
            pairs.append(send(partner, partner_west, 0, east))
            pairs.append(send(partner, partner_north, 1, south))
        pairs.append(send(own.at[part, east_half], received.at[part, east_half], 2 + h, east))
        pairs.append(send(own.at[part, south_half], received.at[part, south_half], 4 + h, south))

    rows_copy.wait()
    index[:, 0:faces] = rows[:, 3 * faces : 4 * faces]
    index[:, faces:two] = rows[:, faces:two]

    @pl.loop(0, 3)
    def _(j):
        n0 = pl.multiple_of(j * wide, wide)
        hot = one_hot(n0, wide, index[:, 0:two])
        spread[:, pl.ds(n0, wide)] = dot_nt(own[...], hot).astype(BF16)

    mask_copy.wait()
    inside = iota((nblock, width), 1) - bsize * iota((nblock, width), 0)
    expanded = dot(
        mask[...].astype(F32).astype(BF16), unit((inside >= 0) & (inside < bsize))
    )
    for i in range(nblock):
        mask_rows[i] = jnp.broadcast_to(expanded[i : i + 1], (16, width)).astype(BF16)

    corner_rows = rows[:, 4 * faces : 4 * faces + four_cd]
    corner_hot = one_hot(0, width, corner_rows)

    @pl.loop(0, chunks)
    def _(j):
        tile_copy(j).wait()
        part = pl.ds(pl.multiple_of(j * tall, tall), tall)
        piece = tile[part].reshape(blocks, group, 16, width)
        piece = piece * mask_rows[pl.ds(j * blocks, blocks)][:, None]
        joint[0:four_cd, part] = dot(piece.reshape(tall, width), corner_hot).T.astype(BF16)

    for f, copy in enumerate(pairs[:2]):
        copy.wait()
        pair_row = (partner_west[0:1], partner_north[1:2])[f]
        face_row = (rows[:, two : 3 * faces], rows[:, 0:faces])[f]
        sub = iota((8, faces), 0)
        digits = jnp.where(sub == 0, face_row >> 8, jnp.where(sub == 1, face_row & 255, 0))
        found = dot(digits.astype(F32).astype(BF16), one_hot(0, faces, pair_row))
        index[:, two + f * faces : two + (f + 1) * faces] = (
            found[0:1] * 256.0 + found[1:2]
        ).astype(I32)
    for copy in pairs[2:6]:
        copy.wait()

    @pl.loop(0, 3)
    def _(j):
        n0 = pl.multiple_of(j * wide, wide)
        hot = one_hot(n0, wide, index[:, two : 2 * two])
        at = (slice(None), pl.ds(n0, wide))
        spread[at] = (spread[at].astype(F32) - dot_nt(received[...], hot)).astype(BF16)

    for copy in basis_copies:
        copy.wait()
    products = dot_nt(joint[...], spread[...]).astype(BF16)
    mine = pl.ds(pl.multiple_of(b * four_cd, 16), four_cd)
    loads[mine] = products[:four_cd]

    def load_copy(k):
        return pltpu.make_async_remote_copy(
            src_ref=loads.at[mine],
            dst_ref=loads.at[mine],
            send_sem=load_send.at[k],
            recv_sem=load_recv.at[k],
            device_id=(a, lax.rem(b + k, ny)),
            device_id_type=MESH,
        )

    pl.loop(1, ny)(lambda k: load_copy(k).start())

    mine_a = pl.ds(pl.multiple_of(a * four_cd, 16), four_cd)
    bilinear[mine_a] = products[four_cd:]

    def bil_copy(k):
        return pltpu.make_async_remote_copy(
            src_ref=bilinear.at[mine_a],
            dst_ref=bilinear.at[mine_a],
            send_sem=bil_send.at[k],
            recv_sem=bil_recv.at[k],
            device_id=(lax.rem(a + k, nx), b),
            device_id_type=MESH,
        )

    pl.loop(1, nx)(lambda k: bil_copy(k).start())

    product[...] = jnp.zeros_like(product)

    @pl.loop(0, 3)
    def _(j):
        at = (slice(None), pl.ds(pl.multiple_of(j * wide, wide), wide))
        masked = tile[at].reshape(nblock, group, 16, wide) * mask_rows[:, :, at[1]][:, None]
        full = dot(spread[...], masked.reshape(width, wide))
        image[0:nrhs, at[1]] = full.astype(BF16)
        full = full * spread[at].astype(F32)
        total = product[...]
        for q in range(wide // 128):
            total = total + full[:, q * 128 : (q + 1) * 128]
        product[...] = total

    def gathered(first, count):
        both = dot(image[...], one_hot(0, width, index[:, first : first + count])).astype(BF16)
        return both[:nrhs], both[nrhs:]

    face_out[:, 0:faces], basis_out[:, 0:faces] = gathered(two, faces)
    pairs.append(send(face_out.at[:, east_half], face_in.at[:, east_half], 6, west))

    for copy in inverse_copies:
        copy.wait()
    total = inverse.shape[1]

    def over(value, count):
        return jnp.where(value >= count, value - count, value)

    def divided(value):
        return (value * (-(-(1 << 19) // cd))) >> 19

    load_at = iota((1, ny * four_cd), 1)
    unit_at = divided(load_at)
    corner = unit_at & 3
    source = (corner >> 1) * row_cd + over((unit_at >> 2) + (corner & 1), ny) * cd
    source = source + load_at - unit_at * cd
    widen = unit(iota((2 * row_cd, ny * four_cd), 0) == source)
    nodes_cd = 8 * cd
    out = iota((nx * nodes_cd, 1), 0)
    unit_at = divided(out)
    place = unit_at & 7
    down = jnp.where(place < 4, place >> 1, jnp.where(place < 6, place - 4, 2))
    along = jnp.where(place < 4, place & 1, jnp.where(place < 6, 2, place - 6))
    node = over((unit_at >> 3) + down, nx) * ny + over(b + along, ny)
    column = node * cd + out - unit_at * cd
    chosen = unit(iota((nx * nodes_cd, total), 1) == column)
    solve[...] = dot(dot_nt(chosen, inverse[...]).astype(BF16), widen).astype(BF16)

    pl.loop(1, ny)(lambda k: load_copy(k).wait())
    solution_part = dot(solve[...], loads[...])
    parts[...] = solution_part.astype(BF16)

    def part_copy(k):
        to = lax.rem(a + k, nx)
        return pltpu.make_async_remote_copy(
            src_ref=parts.at[pl.ds(pl.multiple_of(to * nodes_cd, 16), nodes_cd)],
            dst_ref=parts_in.at[k],
            send_sem=part_send.at[k],
            recv_sem=part_recv.at[k],
            device_id=(to, b),
            device_id_type=MESH,
        )

    pl.loop(1, nx)(lambda k: part_copy(k).start())

    pl.loop(1, nx)(lambda k: bil_copy(k).wait())
    at_corners = solution_part.reshape(nx, nodes_cd, nrhs)[:, :four_cd].reshape(nx * four_cd, nrhs)
    coarse = jnp.sum(at_corners * bilinear[...].astype(F32), axis=0, keepdims=True)
    fine = lax.dot_general(
        jnp.ones((8, 128), F32), product[...], NT, precision=lax.Precision.HIGHEST, preferred_element_type=F32
    )
    mine_y = pl.ds(pl.multiple_of(b * 8, 8), 8)
    sum_y[mine_y] = fine - coarse

    def sumy_copy(k):
        return pltpu.make_async_remote_copy(
            src_ref=sum_y.at[mine_y],
            dst_ref=sum_y.at[mine_y],
            send_sem=sumy_send.at[k],
            recv_sem=sumy_recv.at[k],
            device_id=(a, lax.rem(b + k, ny)),
            device_id_type=MESH,
        )

    pl.loop(1, ny)(lambda k: sumy_copy(k).start())

    face_out[:, faces:two], basis_out[:, faces:two] = gathered(two + faces, faces)
    pairs.append(send(face_out.at[:, south_half], face_in.at[:, south_half], 7, north))
    theirs = pl.ds(four_cd, four_cd)
    pairs.append(send(basis_out.at[:, east_half], stack.at[theirs, east_half], 8, west))
    pairs.append(send(basis_out.at[:, south_half], stack.at[theirs, south_half], 9, north))
    face_own[...], stack[0:four_cd] = gathered(0, two)
    pl.loop(1, ny)(lambda k: sumy_copy(k).wait())
    mine_x = pl.ds(pl.multiple_of(a * 8, 8), 8)
    sum_x[mine_x] = jnp.sum(sum_y[...].reshape(ny, 8, nrhs), axis=0)

    def sumx_copy(k):
        return pltpu.make_async_remote_copy(
            src_ref=sum_x.at[mine_x],
            dst_ref=sum_x.at[mine_x],
            send_sem=sumx_send.at[k],
            recv_sem=sumx_recv.at[k],
            device_id=(lax.rem(a + k, nx), b),
            device_id_type=MESH,
        )

    pl.loop(1, nx)(lambda k: sumx_copy(k).start())

    nodes = parts[pl.ds(pl.multiple_of(a * nodes_cd, 16), nodes_cd)].astype(F32)
    for k in range(1, nx):
        part_copy(k).wait()
        nodes = nodes + parts_in[k].astype(F32)
    nodes = nodes.T.astype(BF16)
    pairs[8].wait()
    pairs[9].wait()
    corrections = []
    for f in range(2):
        row = iota((nodes_cd, 1), 0)
        unit_at = divided(row)
        corner = unit_at & 3
        beyond = (
            jnp.where(corner & 1 == 0, 1 + corner, 4 + (corner >> 1)),
            jnp.where(corner < 2, 2 + corner, 4 + corner),
        )[f]
        place = jnp.where(unit_at < 4, corner, beyond)
        hit = iota((nodes_cd, nodes_cd), 1) == place * cd + row - unit_at * cd
        pick = jnp.where(row < four_cd, 1.0, -1.0) * jnp.where(hit, 1.0, 0.0)
        coefficient = dot_nt(nodes, pick.astype(BF16)).astype(BF16)
        corrections.append(dot(coefficient, stack[:, f * faces : (f + 1) * faces]))

    pl.loop(1, nx)(lambda k: sumx_copy(k).wait())
    everything = jnp.sum(sum_x[...].reshape(nx, 8, nrhs), axis=0)
    curvature_ref[...] = everything[0:1] / (2.0 * faces * nx * ny)

    pairs[7].wait()
    pairs[6].wait()
    for f in range(2):
        at = (slice(None), slice(f * faces, (f + 1) * faces))
        jump = face_own[at].astype(F32) - face_in[at].astype(F32) - corrections[f]
        jump_ref[at] = jump.astype(BF16)


def finish(jump, curvature, jumps_ref, curvature_ref):
    nrhs = jump.shape[0]
    faces = jump.shape[1] // 2
    half = nrhs // 2
    at_row, at_column = iota((nrhs, nrhs), 0), iota((nrhs, nrhs), 1)
    lay = unit(at_row == jnp.where(at_column < half, 2 * at_column, 2 * (at_column - half) + 1))
    for h in range(2):
        part = slice(h * half, (h + 1) * half)
        apart = jnp.concatenate([jump[part, :faces], jump[part, faces:]], axis=0)
        jumps_ref[part] = dot(lay, apart).astype(BF16).reshape(half, 2, faces)
    curvature_ref[...] = curvature[...]


def shards(multipliers, partner, interface_rows, block_mask, tiles, basis, coarse_inverse):
    nx = lax.axis_size("gx")
    ny = lax.axis_size("gy")
    lam = multipliers[0, 0]
    nrhs, _, faces = lam.shape
    rows = interface_rows[0]
    width = tiles.shape[2]
    nblock = block_mask.shape[2]
    four_cd = basis.shape[2]
    total = coarse_inverse.shape[1]
    row_cd = total // nx
    dma = pltpu.SemaphoreType.DMA
    vmem = pltpu.VMEM
    two = 2 * faces
    jump, curvature = pl.pallas_call(
        functools.partial(kernel, nx, ny),
        out_shape=(
            jax.ShapeDtypeStruct((nrhs, two), BF16),
            jax.ShapeDtypeStruct((1, nrhs), F32),
        ),
        in_specs=[pl.BlockSpec(memory_space=pl.ANY)] * 7,
        out_specs=(pl.BlockSpec(memory_space=vmem), pl.BlockSpec(memory_space=vmem)),
        scratch_shapes=[
            vmem(lam.shape, BF16),
            vmem((2, faces), I32),
            vmem(rows.shape, I32),
            vmem((nblock, nblock), I32),
            vmem((width, width), BF16),
            vmem((2 * four_cd, width), BF16),
            vmem((2 * row_cd, total), BF16),
            vmem((nrhs, two), BF16),
            vmem((nrhs, two), BF16),
            vmem((2, faces), I32),
            vmem((2, faces), I32),
            vmem((1, 2 * two), I32),
            vmem((nrhs, width), BF16),
            vmem((nrhs, 128), F32),
            vmem((nrhs + four_cd, width), BF16),
            vmem((nblock, 16, width), BF16),
            vmem((2 * nx * four_cd, ny * four_cd), BF16),
            vmem((ny * four_cd, nrhs), BF16),
            vmem((nx * four_cd, nrhs), BF16),
            vmem((2 * four_cd, two), BF16),
            vmem((four_cd, two), BF16),
            vmem((2 * nx * four_cd, nrhs), BF16),
            vmem((nx, 2 * four_cd, nrhs), BF16),
            vmem((nrhs, two), BF16),
            vmem((nrhs, two), BF16),
            vmem((nrhs, two), BF16),
            vmem((nx * 8, nrhs), F32),
            vmem((ny * 8, nrhs), F32),
            dma((13,)),
            dma((10,)),
            dma((10,)),
            dma((ny,)),
            dma((ny,)),
            dma((nx,)),
            dma((nx,)),
            dma((nx,)),
            dma((nx,)),
            dma((nx,)),
            dma((nx,)),
            dma((ny,)),
            dma((ny,)),
        ],
        compiler_params=pltpu.CompilerParams(
            collective_id=0, has_side_effects=True, vmem_limit_bytes=60 * 2**20
        ),
    )(lam, partner[0, 0], rows, block_mask[0, 0], tiles[0, 0], basis[0, 0], coarse_inverse)
    jumps, curvature = pl.pallas_call(
        finish,
        out_shape=(jax.ShapeDtypeStruct(lam.shape, BF16), jax.ShapeDtypeStruct((1, nrhs), F32)),
        in_specs=[pl.BlockSpec(memory_space=vmem)] * 2,
        out_specs=(pl.BlockSpec(memory_space=vmem), pl.BlockSpec(memory_space=vmem)),
    )(jump, curvature)
    return jumps[None, None], curvature.reshape(nrhs)


def solution(mesh):
    in_specs = (
        P("gx", "gy", None, None, None),
        P("gx", "gy", None, None),
        P("gx", "gy", None),
        P("gx", "gy", None, None),
        P("gx", "gy", None, None),
        P("gx", "gy", None, None),
        P(),
    )
    out_specs = (P("gx", "gy", None, None, None), P())
    return jax.shard_map(shards, mesh=mesh, in_specs=in_specs, out_specs=out_specs, check_vma=False)
```

```python
import functools

import jax
import jax.numpy as jnp
from jax import lax
from jax.experimental import pallas as pl
from jax.experimental.pallas import tpu as pltpu
from jax.sharding import PartitionSpec as P

MESH = pl.DeviceIdType.MESH
BF16 = jnp.bfloat16
F32 = jnp.float32
I32 = jnp.int32
NT = (((1,), (1,)), ((), ()))


def dot(x, y):
    return jnp.dot(x, y, preferred_element_type=F32)


def dot_nt(x, y):
    return lax.dot_general(x, y, NT, preferred_element_type=F32)


def iota(shape, dim):
    return lax.broadcasted_iota(I32, shape, dim)


def unit(cond):
    return jnp.where(cond, jnp.ones((), BF16), jnp.zeros((), BF16))


def one_hot(first, count, index):
    rows = iota((count, index.shape[1]), 0).astype(jnp.int16)
    return unit(rows == (index - first).astype(jnp.int16))


def kernel(
    nx,
    ny,
    lam_hbm,
    partner_hbm,
    rows_hbm,
    mask_hbm,
    tile_hbm,
    basis_hbm,
    inverse_hbm,
    jump_ref,
    curvature_ref,
    lam,
    partner,
    rows,
    mask,
    tile,
    joint,
    inverse,
    own,
    received,
    partner_west,
    partner_north,
    index,
    spread,
    product,
    image,
    mask_rows,
    solve,
    loads,
    bilinear,
    stack,
    basis_out,
    parts,
    parts_in,
    face_out,
    face_in,
    face_own,
    sum_x,
    sum_y,
    local_sem,
    pair_send,
    pair_recv,
    load_send,
    load_recv,
    bil_send,
    bil_recv,
    part_send,
    part_recv,
    sumx_send,
    sumx_recv,
    sumy_send,
    sumy_recv,
):
    a = lax.axis_index("gx")
    b = lax.axis_index("gy")
    nrhs, _, faces = lam.shape
    width = tile.shape[0]
    nblock = mask.shape[0]
    bsize = width // nblock
    group = bsize // 16
    four_cd = basis_hbm.shape[0]
    cd = four_cd // 4
    row_cd = ny * cd
    two = 2 * faces
    first_piece = faces * 2 // 5 // 128 * 128
    chunks = 4
    tall = width // chunks
    blocks = nblock // chunks
    wide = width // 3
    east = (a, lax.rem(b + 1, ny))
    west = (a, lax.rem(b + ny - 1, ny))
    south = (lax.rem(a + 1, nx), b)
    north = (lax.rem(a + nx - 1, nx), b)

    def fetch(src, dst, slot):
        copy = pltpu.make_async_copy(src, dst, local_sem.at[slot])
        copy.start()
        return copy

    half = nrhs // 2
    lam_copies = [
        fetch(lam_hbm.at[pl.ds(h * half, half)], lam.at[pl.ds(h * half, half)], (0, 7)[h]) for h in range(2)
    ]
    rows_copy = fetch(rows_hbm, rows, 1)
    partner_copy = fetch(partner_hbm, partner, 2)
    mask_copy = fetch(mask_hbm, mask, 3)

    def tile_copy(j):
        part = pl.ds(pl.multiple_of(j * tall, tall), tall)
        return pltpu.make_async_copy(tile_hbm.at[part], tile.at[part], local_sem.at[8 + j])

    barrier = pltpu.get_barrier_semaphore()

    @pl.loop(1, ny)
    def _(k):
        pl.semaphore_signal(barrier, inc=1, device_id=(a, lax.rem(b + k, ny)), device_id_type=MESH)

    @pl.loop(1, nx)
    def _(k):
        pl.semaphore_signal(barrier, inc=1, device_id=(lax.rem(a + k, nx), b), device_id_type=MESH)

    for j in range(chunks):
        tile_copy(j).start()
    basis_rows = pl.ds(nrhs, four_cd)
    basis_copies = [
        fetch(basis_hbm, joint.at[pl.ds(four_cd, four_cd)], 4),
        fetch(basis_hbm, image.at[basis_rows], 12),
    ]
    inverse_copies = []
    for p in range(2):
        first = pl.multiple_of(lax.rem(a + p, nx) * row_cd, 16)
        inverse_copies.append(
            fetch(inverse_hbm.at[pl.ds(first, row_cd)], inverse.at[pl.ds(p * row_cd, row_cd)], 5 + p)
        )

    def send(src, dst, slot, device):
        copy = pltpu.make_async_remote_copy(
            src_ref=src,
            dst_ref=dst,
            send_sem=pair_send.at[slot],
            recv_sem=pair_recv.at[slot],
            device_id=device,
            device_id_type=MESH,
        )
        copy.start()
        return copy

    east_half = pl.ds(0, faces)
    south_half = pl.ds(faces, faces)
    at_row, at_column = iota((nrhs, nrhs), 0), iota((nrhs, nrhs), 1)
    pick = unit(at_column == jnp.where(at_row < half, 2 * at_row, 2 * (at_row - half) + 1))
    pairs = []
    for h in range(2):
        part = pl.ds(h * half, half)
        lam_copies[h].wait()
        apart = dot(pick, lam[part].reshape(nrhs, faces)).astype(BF16)
        own[part, 0:faces] = apart[:half]
        own[part, faces:two] = apart[half:]
        if h == 0:
            partner_copy.wait()
            pl.semaphore_wait(barrier, nx + ny - 2)
            pairs.append(send(partner, partner_west, 0, east))
            pairs.append(send(partner, partner_north, 1, south))
        pairs.append(send(own.at[part, east_half], received.at[part, east_half], 2 + h, east))
        pairs.append(send(own.at[part, south_half], received.at[part, south_half], 4 + h, south))

    rows_copy.wait()
    index[:, 0:faces] = rows[:, 3 * faces : 4 * faces]
    index[:, faces:two] = rows[:, faces:two]

    @pl.loop(0, 3)
    def _(j):
        n0 = pl.multiple_of(j * wide, wide)
        hot = one_hot(n0, wide, index[:, 0:two])
        spread[:, pl.ds(n0, wide)] = dot_nt(own[...], hot).astype(BF16)

    mask_copy.wait()
    inside = iota((nblock, width), 1) - bsize * iota((nblock, width), 0)
    expanded = dot(
        mask[...].astype(F32).astype(BF16), unit((inside >= 0) & (inside < bsize))
    )
    for i in range(nblock):
        mask_rows[i] = jnp.broadcast_to(expanded[i : i + 1], (16, width)).astype(BF16)

    corner_rows = rows[:, 4 * faces : 4 * faces + four_cd]
    corner_hot = one_hot(0, width, corner_rows)

    @pl.loop(0, chunks)
    def _(j):
        tile_copy(j).wait()
        part = pl.ds(pl.multiple_of(j * tall, tall), tall)
        piece = tile[part].reshape(blocks, group, 16, width)
        piece = piece * mask_rows[pl.ds(j * blocks, blocks)][:, None]
        joint[0:four_cd, part] = dot(piece.reshape(tall, width), corner_hot).T.astype(BF16)

    for copy in inverse_copies:
        copy.wait()
    total = inverse.shape[1]

    def over(value, count):
        return jnp.where(value >= count, value - count, value)

    def divided(value):
        return (value * (-(-(1 << 19) // cd))) >> 19

    load_at = iota((1, ny * four_cd), 1)
    unit_at = divided(load_at)
    corner = unit_at & 3
    source = (corner >> 1) * row_cd + over((unit_at >> 2) + (corner & 1), ny) * cd
    source = source + load_at - unit_at * cd
    widen = unit(iota((2 * row_cd, ny * four_cd), 0) == source)
    nodes_cd = 8 * cd
    out = iota((nx * nodes_cd, 1), 0)
    unit_at = divided(out)
    place = unit_at & 7
    down = jnp.where(place < 4, place >> 1, jnp.where(place < 6, place - 4, 2))
    along = jnp.where(place < 4, place & 1, jnp.where(place < 6, 2, place - 6))
    node = over((unit_at >> 3) + down, nx) * ny + over(b + along, ny)
    column = node * cd + out - unit_at * cd
    chosen = unit(iota((nx * nodes_cd, total), 1) == column)
    solve[...] = dot(dot_nt(chosen, inverse[...]).astype(BF16), widen).astype(BF16)

    for f, copy in enumerate(pairs[:2]):
        copy.wait()
        pair_row = (partner_west[0:1], partner_north[1:2])[f]
        face_row = (rows[:, two : 3 * faces], rows[:, 0:faces])[f]
        sub = iota((8, faces), 0)
        digits = jnp.where(sub == 0, face_row >> 8, jnp.where(sub == 1, face_row & 255, 0))
        found = dot(digits.astype(F32).astype(BF16), one_hot(0, faces, pair_row))
        index[:, two + f * faces : two + (f + 1) * faces] = (
            found[0:1] * 256.0 + found[1:2]
        ).astype(I32)
    for copy in pairs[2:6]:
        copy.wait()

    @pl.loop(0, 3)
    def _(j):
        n0 = pl.multiple_of(j * wide, wide)
        hot = one_hot(n0, wide, index[:, two : 2 * two])
        at = (slice(None), pl.ds(n0, wide))
        spread[at] = (spread[at].astype(F32) - dot_nt(received[...], hot)).astype(BF16)

    for copy in basis_copies:
        copy.wait()
    products = dot_nt(joint[...], spread[...]).astype(BF16)
    mine = pl.ds(pl.multiple_of(b * four_cd, 16), four_cd)
    loads[mine] = products[:four_cd]

    def load_copy(k):
        return pltpu.make_async_remote_copy(
            src_ref=loads.at[mine],
            dst_ref=loads.at[mine],
            send_sem=load_send.at[k],
            recv_sem=load_recv.at[k],
            device_id=(a, lax.rem(b + k, ny)),
            device_id_type=MESH,
        )

    pl.loop(1, ny)(lambda k: load_copy(k).start())

    mine_a = pl.ds(pl.multiple_of(a * four_cd, 16), four_cd)
    bilinear[mine_a] = products[four_cd:]

    def bil_copy(k):
        return pltpu.make_async_remote_copy(
            src_ref=bilinear.at[mine_a],
            dst_ref=bilinear.at[mine_a],
            send_sem=bil_send.at[k],
            recv_sem=bil_recv.at[k],
            device_id=(lax.rem(a + k, nx), b),
            device_id_type=MESH,
        )

    pl.loop(1, nx)(lambda k: bil_copy(k).start())

    product[...] = jnp.zeros_like(product)

    @pl.loop(0, 3)
    def _(j):
        at = (slice(None), pl.ds(pl.multiple_of(j * wide, wide), wide))
        masked = tile[at].reshape(nblock, group, 16, wide) * mask_rows[:, :, at[1]][:, None]
        full = dot(spread[...], masked.reshape(width, wide))
        image[0:nrhs, at[1]] = full.astype(BF16)
        full = full * spread[at].astype(F32)
        total = product[...]
        for q in range(wide // 128):
            total = total + full[:, q * 128 : (q + 1) * 128]
        product[...] = total

    pl.loop(1, ny)(lambda k: load_copy(k).wait())
    solution_part = dot(solve[...], loads[...])
    parts[...] = solution_part.astype(BF16)

    def part_copy(k):
        to = lax.rem(a + k, nx)
        return pltpu.make_async_remote_copy(
            src_ref=parts.at[pl.ds(pl.multiple_of(to * nodes_cd, 16), nodes_cd)],
            dst_ref=parts_in.at[k],
            send_sem=part_send.at[k],
            recv_sem=part_recv.at[k],
            device_id=(to, b),
            device_id_type=MESH,
        )

    pl.loop(1, nx)(lambda k: part_copy(k).start())

    pl.loop(1, nx)(lambda k: bil_copy(k).wait())
    at_corners = solution_part.reshape(nx, nodes_cd, nrhs)[:, :four_cd].reshape(nx * four_cd, nrhs)
    coarse = jnp.sum(at_corners * bilinear[...].astype(F32), axis=0, keepdims=True)
    fine = lax.dot_general(
        jnp.ones((8, 128), F32), product[...], NT, precision=lax.Precision.HIGHEST, preferred_element_type=F32
    )
    sum_y[b] = (fine - coarse)[0:1]

    def sumy_copy(k):
        return pltpu.make_async_remote_copy(
            src_ref=sum_y.at[b],
            dst_ref=sum_y.at[b],
            send_sem=sumy_send.at[k],
            recv_sem=sumy_recv.at[k],
            device_id=(a, lax.rem(b + k, ny)),
            device_id_type=MESH,
        )

    pl.loop(1, ny)(lambda k: sumy_copy(k).start())

    def gathered(first, count):
        both = dot(image[...], one_hot(0, width, index[:, first : first + count])).astype(BF16)
        return both[:nrhs], both[nrhs:]

    west_pieces = []
    for slot, first, count in ((10, 0, first_piece), (6, first_piece, faces - first_piece)):
        at = (slice(None), slice(first, first + count))
        face_out[at], basis_out[at] = gathered(two + first, count)
        at = (slice(None), pl.ds(first, count))
        west_pieces.append(send(face_out.at[at], face_in.at[at], slot, west))
    pairs.append(west_pieces[1])

    face_out[:, faces:two], basis_out[:, faces:two] = gathered(two + faces, faces)
    pairs.append(send(face_out.at[:, south_half], face_in.at[:, south_half], 7, north))
    theirs = pl.ds(four_cd, four_cd)
    pairs.append(send(basis_out.at[:, east_half], stack.at[theirs, east_half], 8, west))
    pairs.append(send(basis_out.at[:, south_half], stack.at[theirs, south_half], 9, north))
    face_own[...], stack[0:four_cd] = gathered(0, two)
    pl.loop(1, ny)(lambda k: sumy_copy(k).wait())
    sum_x[a] = jnp.sum(sum_y[...], axis=0)

    def sumx_copy(k):
        return pltpu.make_async_remote_copy(
            src_ref=sum_x.at[a],
            dst_ref=sum_x.at[a],
            send_sem=sumx_send.at[k],
            recv_sem=sumx_recv.at[k],
            device_id=(lax.rem(a + k, nx), b),
            device_id_type=MESH,
        )

    pl.loop(1, nx)(lambda k: sumx_copy(k).start())

    nodes = parts[pl.ds(pl.multiple_of(a * nodes_cd, 16), nodes_cd)].astype(F32)
    for k in range(1, nx):
        part_copy(k).wait()
        nodes = nodes + parts_in[k].astype(F32)
    nodes = nodes.T.astype(BF16)
    pairs[8].wait()
    pairs[9].wait()
    corrections = []
    for f in range(2):
        row = iota((nodes_cd, 1), 0)
        unit_at = divided(row)
        corner = unit_at & 3
        beyond = (
            jnp.where(corner & 1 == 0, 1 + corner, 4 + (corner >> 1)),
            jnp.where(corner < 2, 2 + corner, 4 + corner),
        )[f]
        place = jnp.where(unit_at < 4, corner, beyond)
        hit = iota((nodes_cd, nodes_cd), 1) == place * cd + row - unit_at * cd
        pick = jnp.where(row < four_cd, 1.0, -1.0) * jnp.where(hit, 1.0, 0.0)
        coefficient = dot_nt(nodes, pick.astype(BF16)).astype(BF16)
        corrections.append(dot(coefficient, stack[:, f * faces : (f + 1) * faces]))

    pl.loop(1, nx)(lambda k: sumx_copy(k).wait())
    curvature_ref[...] = jnp.sum(sum_x[...], axis=0) / (2.0 * faces * nx * ny)

    pairs[7].wait()
    west_pieces[0].wait()
    pairs[6].wait()
    for f in range(2):
        at = (slice(None), slice(f * faces, (f + 1) * faces))
        jump = face_own[at].astype(F32) - face_in[at].astype(F32) - corrections[f]
        jump_ref[at] = jump.astype(BF16)


def finish(jump, curvature, jumps_ref, curvature_ref):
    nrhs = jump.shape[0]
    faces = jump.shape[1] // 2
    half = nrhs // 2
    at_row, at_column = iota((nrhs, nrhs), 0), iota((nrhs, nrhs), 1)
    lay = unit(at_row == jnp.where(at_column < half, 2 * at_column, 2 * (at_column - half) + 1))
    for h in range(2):
        part = slice(h * half, (h + 1) * half)
        apart = jnp.concatenate([jump[part, :faces], jump[part, faces:]], axis=0)
        jumps_ref[part] = dot(lay, apart).astype(BF16).reshape(half, 2, faces)
    curvature_ref[...] = curvature[...]


def shards(multipliers, partner, interface_rows, block_mask, tiles, basis, coarse_inverse):
    nx = lax.axis_size("gx")
    ny = lax.axis_size("gy")
    lam = multipliers[0, 0]
    nrhs, _, faces = lam.shape
    rows = interface_rows[0]
    width = tiles.shape[2]
    nblock = block_mask.shape[2]
    four_cd = basis.shape[2]
    total = coarse_inverse.shape[1]
    row_cd = total // nx
    dma = pltpu.SemaphoreType.DMA
    vmem = pltpu.VMEM
    two = 2 * faces
    jump, curvature = pl.pallas_call(
        functools.partial(kernel, nx, ny),
        out_shape=(
            jax.ShapeDtypeStruct((nrhs, two), BF16),
            jax.ShapeDtypeStruct((1, nrhs), F32),
        ),
        in_specs=[pl.BlockSpec(memory_space=pl.ANY)] * 7,
        out_specs=(pl.BlockSpec(memory_space=vmem), pl.BlockSpec(memory_space=vmem)),
        scratch_shapes=[
            vmem(lam.shape, BF16),
            vmem((2, faces), I32),
            vmem(rows.shape, I32),
            vmem((nblock, nblock), I32),
            vmem((width, width), BF16),
            vmem((2 * four_cd, width), BF16),
            vmem((2 * row_cd, total), BF16),
            vmem((nrhs, two), BF16),
            vmem((nrhs, two), BF16),
            vmem((2, faces), I32),
            vmem((2, faces), I32),
            vmem((1, 2 * two), I32),
            vmem((nrhs, width), BF16),
            vmem((nrhs, 128), F32),
            vmem((nrhs + four_cd, width), BF16),
            vmem((nblock, 16, width), BF16),
            vmem((2 * nx * four_cd, ny * four_cd), BF16),
            vmem((ny * four_cd, nrhs), BF16),
            vmem((nx * four_cd, nrhs), BF16),
            vmem((2 * four_cd, two), BF16),
            vmem((four_cd, two), BF16),
            vmem((2 * nx * four_cd, nrhs), BF16),
            vmem((nx, 2 * four_cd, nrhs), BF16),
            vmem((nrhs, two), BF16),
            vmem((nrhs, two), BF16),
            vmem((nrhs, two), BF16),
            vmem((nx, 1, nrhs), F32),
            vmem((ny, 1, nrhs), F32),
            dma((13,)),
            dma((11,)),
            dma((11,)),
            dma((ny,)),
            dma((ny,)),
            dma((nx,)),
            dma((nx,)),
            dma((nx,)),
            dma((nx,)),
            dma((nx,)),
            dma((nx,)),
            dma((ny,)),
            dma((ny,)),
        ],
        compiler_params=pltpu.CompilerParams(
            collective_id=0, has_side_effects=True, vmem_limit_bytes=60 * 2**20
        ),
    )(lam, partner[0, 0], rows, block_mask[0, 0], tiles[0, 0], basis[0, 0], coarse_inverse)
    jumps, curvature = pl.pallas_call(
        finish,
        out_shape=(jax.ShapeDtypeStruct(lam.shape, BF16), jax.ShapeDtypeStruct((1, nrhs), F32)),
        in_specs=[pl.BlockSpec(memory_space=vmem)] * 2,
        out_specs=(pl.BlockSpec(memory_space=vmem), pl.BlockSpec(memory_space=vmem)),
    )(jump, curvature)
    return jumps[None, None], curvature.reshape(nrhs)


def solution(mesh):
    in_specs = (
        P("gx", "gy", None, None, None),
        P("gx", "gy", None, None),
        P("gx", "gy", None),
        P("gx", "gy", None, None),
        P("gx", "gy", None, None),
        P("gx", "gy", None, None),
        P(),
    )
    out_specs = (P("gx", "gy", None, None, None), P())
    return jax.shard_map(shards, mesh=mesh, in_specs=in_specs, out_specs=out_specs, check_vma=False)
```

```python
import functools

import jax
import jax.numpy as jnp
from jax import lax
from jax.experimental import pallas as pl
from jax.experimental.pallas import tpu as pltpu
from jax.sharding import PartitionSpec as P

MESH = pl.DeviceIdType.MESH
BF16 = jnp.bfloat16
F32 = jnp.float32
I32 = jnp.int32
NT = (((1,), (1,)), ((), ()))


def dot(x, y):
    return jnp.dot(x, y, preferred_element_type=F32)


def dot_nt(x, y):
    return lax.dot_general(x, y, NT, preferred_element_type=F32)


def iota(shape, dim):
    return lax.broadcasted_iota(I32, shape, dim)


def unit(cond):
    return jnp.where(cond, jnp.ones((), BF16), jnp.zeros((), BF16))


def one_hot(first, count, index):
    rows = iota((count, index.shape[1]), 0).astype(jnp.int16)
    return unit(rows == (index - first).astype(jnp.int16))


def kernel(
    nx,
    ny,
    lam_hbm,
    partner_hbm,
    rows_hbm,
    mask_hbm,
    tile_hbm,
    basis_hbm,
    inverse_hbm,
    jump_ref,
    curvature_ref,
    lam,
    partner,
    rows,
    mask,
    tile,
    joint,
    inverse,
    own,
    received,
    partner_west,
    partner_north,
    index,
    spread,
    product,
    image,
    mask_rows,
    solve,
    loads,
    bilinear,
    stack,
    basis_out,
    parts,
    parts_in,
    face_out,
    face_in,
    face_own,
    sum_x,
    sum_y,
    local_sem,
    pair_send,
    pair_recv,
    load_send,
    load_recv,
    bil_send,
    bil_recv,
    part_send,
    part_recv,
    sumx_send,
    sumx_recv,
    sumy_send,
    sumy_recv,
):
    a = lax.axis_index("gx")
    b = lax.axis_index("gy")
    nrhs, _, faces = lam.shape
    width = tile.shape[0]
    nblock = mask.shape[0]
    bsize = width // nblock
    group = bsize // 16
    four_cd = basis_hbm.shape[0]
    cd = four_cd // 4
    row_cd = ny * cd
    two = 2 * faces
    first_piece = faces * 2 // 5 // 128 * 128
    chunks = 4
    tall = width // chunks
    blocks = nblock // chunks
    wide = width // 3
    east = (a, lax.rem(b + 1, ny))
    west = (a, lax.rem(b + ny - 1, ny))
    south = (lax.rem(a + 1, nx), b)
    north = (lax.rem(a + nx - 1, nx), b)

    def fetch(src, dst, slot):
        copy = pltpu.make_async_copy(src, dst, local_sem.at[slot])
        copy.start()
        return copy

    half = nrhs // 2
    lam_copies = [
        fetch(lam_hbm.at[pl.ds(h * half, half)], lam.at[pl.ds(h * half, half)], (0, 7)[h]) for h in range(2)
    ]
    rows_copy = fetch(rows_hbm, rows, 1)
    partner_copy = fetch(partner_hbm, partner, 2)
    mask_copy = fetch(mask_hbm, mask, 3)

    def tile_copy(j):
        part = pl.ds(pl.multiple_of(j * tall, tall), tall)
        return pltpu.make_async_copy(tile_hbm.at[part], tile.at[part], local_sem.at[8 + j])

    barrier = pltpu.get_barrier_semaphore()

    @pl.loop(1, ny)
    def _(k):
        pl.semaphore_signal(barrier, inc=1, device_id=(a, lax.rem(b + k, ny)), device_id_type=MESH)

    @pl.loop(1, nx)
    def _(k):
        pl.semaphore_signal(barrier, inc=1, device_id=(lax.rem(a + k, nx), b), device_id_type=MESH)

    for j in range(chunks):
        tile_copy(j).start()
    basis_rows = pl.ds(nrhs, four_cd)
    basis_copies = [
        fetch(basis_hbm, joint.at[pl.ds(four_cd, four_cd)], 4),
        fetch(basis_hbm, image.at[basis_rows], 12),
    ]
    inverse_copies = []
    for p in range(2):
        first = pl.multiple_of(lax.rem(a + p, nx) * row_cd, 16)
        inverse_copies.append(
            fetch(inverse_hbm.at[pl.ds(first, row_cd)], inverse.at[pl.ds(p * row_cd, row_cd)], 5 + p)
        )

    def send(src, dst, slot, device):
        copy = pltpu.make_async_remote_copy(
            src_ref=src,
            dst_ref=dst,
            send_sem=pair_send.at[slot],
            recv_sem=pair_recv.at[slot],
            device_id=device,
            device_id_type=MESH,
        )
        copy.start()
        return copy

    east_half = pl.ds(0, faces)
    south_half = pl.ds(faces, faces)
    at_row, at_column = iota((nrhs, nrhs), 0), iota((nrhs, nrhs), 1)
    pick = unit(at_column == jnp.where(at_row < half, 2 * at_row, 2 * (at_row - half) + 1))
    pairs = []
    for h in range(2):
        part = pl.ds(h * half, half)
        lam_copies[h].wait()
        apart = dot(pick, lam[part].reshape(nrhs, faces)).astype(BF16)
        own[part, 0:faces] = apart[:half]
        own[part, faces:two] = apart[half:]
        if h == 0:
            partner_copy.wait()
            pl.semaphore_wait(barrier, nx + ny - 2)
            pairs.append(send(partner, partner_west, 0, east))
            pairs.append(send(partner, partner_north, 1, south))
        pairs.append(send(own.at[part, east_half], received.at[part, east_half], 2 + h, east))
        pairs.append(send(own.at[part, south_half], received.at[part, south_half], 4 + h, south))

    rows_copy.wait()
    index[:, 0:faces] = rows[:, 3 * faces : 4 * faces]
    index[:, faces:two] = rows[:, faces:two]

    @pl.loop(0, 3)
    def _(j):
        n0 = pl.multiple_of(j * wide, wide)
        hot = one_hot(n0, wide, index[:, 0:two])
        spread[:, pl.ds(n0, wide)] = dot_nt(own[...], hot).astype(BF16)

    mask_copy.wait()
    inside = iota((nblock, width), 1) - bsize * iota((nblock, width), 0)
    expanded = dot(
        mask[...].astype(F32).astype(BF16), unit((inside >= 0) & (inside < bsize))
    )
    for i in range(nblock):
        mask_rows[i] = jnp.broadcast_to(expanded[i : i + 1], (16, width)).astype(BF16)

    corner_rows = rows[:, 4 * faces : 4 * faces + four_cd]
    corner_hot = one_hot(0, width, corner_rows)

    @pl.loop(0, chunks)
    def _(j):
        tile_copy(j).wait()
        part = pl.ds(pl.multiple_of(j * tall, tall), tall)
        piece = tile[part].reshape(blocks, group, 16, width)
        piece = piece * mask_rows[pl.ds(j * blocks, blocks)][:, None]
        joint[0:four_cd, part] = dot(piece.reshape(tall, width), corner_hot).T.astype(BF16)

    for copy in inverse_copies:
        copy.wait()
    total = inverse.shape[1]

    def over(value, count):
        return jnp.where(value >= count, value - count, value)

    def divided(value):
        return (value * (-(-(1 << 19) // cd))) >> 19

    load_at = iota((1, ny * four_cd), 1)
    unit_at = divided(load_at)
    corner = unit_at & 3
    source = (corner >> 1) * row_cd + over((unit_at >> 2) + (corner & 1), ny) * cd
    source = source + load_at - unit_at * cd
    widen = unit(iota((2 * row_cd, ny * four_cd), 0) == source)
    nodes_cd = 8 * cd
    out = iota((nx * nodes_cd, 1), 0)
    unit_at = divided(out)
    place = unit_at & 7
    down = jnp.where(place < 4, place >> 1, jnp.where(place < 6, place - 4, 2))
    along = jnp.where(place < 4, place & 1, jnp.where(place < 6, 2, place - 6))
    node = over((unit_at >> 3) + down, nx) * ny + over(b + along, ny)
    column = node * cd + out - unit_at * cd
    chosen = unit(iota((nx * nodes_cd, total), 1) == column)
    solve[...] = dot(dot_nt(chosen, inverse[...]).astype(BF16), widen).astype(BF16)

    for f, copy in enumerate(pairs[:2]):
        copy.wait()
        pair_row = (partner_west[0:1], partner_north[1:2])[f]
        face_row = (rows[:, two : 3 * faces], rows[:, 0:faces])[f]
        sub = iota((8, faces), 0)
        digits = jnp.where(sub == 0, face_row >> 8, jnp.where(sub == 1, face_row & 255, 0))
        found = dot(digits.astype(F32).astype(BF16), one_hot(0, faces, pair_row))
        index[:, two + f * faces : two + (f + 1) * faces] = (
            found[0:1] * 256.0 + found[1:2]
        ).astype(I32)
    for copy in pairs[2:6]:
        copy.wait()

    @pl.loop(0, 3)
    def _(j):
        n0 = pl.multiple_of(j * wide, wide)
        hot = one_hot(n0, wide, index[:, two : 2 * two])
        at = (slice(None), pl.ds(n0, wide))
        spread[at] = (spread[at].astype(F32) - dot_nt(received[...], hot)).astype(BF16)

    for copy in basis_copies:
        copy.wait()
    products = dot_nt(joint[...], spread[...]).astype(BF16)
    mine = pl.ds(pl.multiple_of(b * four_cd, 16), four_cd)
    loads[mine] = products[:four_cd]

    def load_copy(k):
        return pltpu.make_async_remote_copy(
            src_ref=loads.at[mine],
            dst_ref=loads.at[mine],
            send_sem=load_send.at[k],
            recv_sem=load_recv.at[k],
            device_id=(a, lax.rem(b + k, ny)),
            device_id_type=MESH,
        )

    pl.loop(1, ny)(lambda k: load_copy(k).start())

    mine_a = pl.ds(pl.multiple_of(a * four_cd, 16), four_cd)
    bilinear[mine_a] = products[four_cd:]

    def bil_copy(k):
        return pltpu.make_async_remote_copy(
            src_ref=bilinear.at[mine_a],
            dst_ref=bilinear.at[mine_a],
            send_sem=bil_send.at[k],
            recv_sem=bil_recv.at[k],
            device_id=(lax.rem(a + k, nx), b),
            device_id_type=MESH,
        )

    pl.loop(1, nx)(lambda k: bil_copy(k).start())

    product[...] = jnp.zeros_like(product)

    @pl.loop(0, 3)
    def _(j):
        at = (slice(None), pl.ds(pl.multiple_of(j * wide, wide), wide))
        masked = tile[at].reshape(nblock, group, 16, wide) * mask_rows[:, :, at[1]][:, None]
        full = dot(spread[...], masked.reshape(width, wide))
        image[0:nrhs, at[1]] = full.astype(BF16)
        full = full * spread[at].astype(F32)
        total = product[...]
        for q in range(wide // 128):
            total = total + full[:, q * 128 : (q + 1) * 128]
        product[...] = total

    pl.loop(1, ny)(lambda k: load_copy(k).wait())
    solution_part = dot(solve[...], loads[...])
    parts[...] = solution_part.astype(BF16)

    def part_copy(k):
        to = lax.rem(a + k, nx)
        return pltpu.make_async_remote_copy(
            src_ref=parts.at[pl.ds(pl.multiple_of(to * nodes_cd, 16), nodes_cd)],
            dst_ref=parts_in.at[k],
            send_sem=part_send.at[k],
            recv_sem=part_recv.at[k],
            device_id=(to, b),
            device_id_type=MESH,
        )

    pl.loop(1, nx)(lambda k: part_copy(k).start())

    pl.loop(1, nx)(lambda k: bil_copy(k).wait())
    at_corners = solution_part.reshape(nx, nodes_cd, nrhs)[:, :four_cd].reshape(nx * four_cd, nrhs)
    coarse = jnp.sum(at_corners * bilinear[...].astype(F32), axis=0, keepdims=True)
    fine = lax.dot_general(
        jnp.ones((8, 128), F32), product[...], NT, precision=lax.Precision.HIGHEST, preferred_element_type=F32
    )
    sum_y[b] = (fine - coarse)[0:1]

    def sumy_copy(k):
        return pltpu.make_async_remote_copy(
            src_ref=sum_y.at[b],
            dst_ref=sum_y.at[b],
            send_sem=sumy_send.at[k],
            recv_sem=sumy_recv.at[k],
            device_id=(a, lax.rem(b + k, ny)),
            device_id_type=MESH,
        )

    pl.loop(1, ny)(lambda k: sumy_copy(k).start())

    def gathered(first, count):
        both = dot(image[...], one_hot(0, width, index[:, first : first + count])).astype(BF16)
        return both[:nrhs], both[nrhs:]

    west_pieces = []
    for slot, first, count in ((10, 0, first_piece), (6, first_piece, faces - first_piece)):
        at = (slice(None), slice(first, first + count))
        face_out[at], basis_out[at] = gathered(two + first, count)
        at = (slice(None), pl.ds(first, count))
        west_pieces.append(send(face_out.at[at], face_in.at[at], slot, west))
        if first == 0:
            face_out[:, faces:two], basis_out[:, faces:two] = gathered(two + faces, faces)
            north_copy = send(face_out.at[:, south_half], face_in.at[:, south_half], 7, north)
    pairs.append(west_pieces[1])
    pairs.append(north_copy)

    theirs = pl.ds(four_cd, four_cd)
    pairs.append(send(basis_out.at[:, east_half], stack.at[theirs, east_half], 8, west))
    pairs.append(send(basis_out.at[:, south_half], stack.at[theirs, south_half], 9, north))
    face_own[...], stack[0:four_cd] = gathered(0, two)
    pl.loop(1, ny)(lambda k: sumy_copy(k).wait())
    sum_x[a] = jnp.sum(sum_y[...], axis=0)

    def sumx_copy(k):
        return pltpu.make_async_remote_copy(
            src_ref=sum_x.at[a],
            dst_ref=sum_x.at[a],
            send_sem=sumx_send.at[k],
            recv_sem=sumx_recv.at[k],
            device_id=(lax.rem(a + k, nx), b),
            device_id_type=MESH,
        )

    pl.loop(1, nx)(lambda k: sumx_copy(k).start())

    nodes = parts[pl.ds(pl.multiple_of(a * nodes_cd, 16), nodes_cd)].astype(F32)
    for k in range(1, nx):
        part_copy(k).wait()
        nodes = nodes + parts_in[k].astype(F32)
    nodes = nodes.T.astype(BF16)
    pairs[8].wait()
    pairs[9].wait()
    corrections = []
    for f in range(2):
        row = iota((nodes_cd, 1), 0)
        unit_at = divided(row)
        corner = unit_at & 3
        beyond = (
            jnp.where(corner & 1 == 0, 1 + corner, 4 + (corner >> 1)),
            jnp.where(corner < 2, 2 + corner, 4 + corner),
        )[f]
        place = jnp.where(unit_at < 4, corner, beyond)
        hit = iota((nodes_cd, nodes_cd), 1) == place * cd + row - unit_at * cd
        pick = jnp.where(row < four_cd, 1.0, -1.0) * jnp.where(hit, 1.0, 0.0)
        coefficient = dot_nt(nodes, pick.astype(BF16)).astype(BF16)
        corrections.append(dot(coefficient, stack[:, f * faces : (f + 1) * faces]))

    pl.loop(1, nx)(lambda k: sumx_copy(k).wait())
    curvature_ref[...] = jnp.sum(sum_x[...], axis=0) / (2.0 * faces * nx * ny)

    pairs[7].wait()
    west_pieces[0].wait()
    pairs[6].wait()
    for f in range(2):
        at = (slice(None), slice(f * faces, (f + 1) * faces))
        jump = face_own[at].astype(F32) - face_in[at].astype(F32) - corrections[f]
        jump_ref[at] = jump.astype(BF16)


def finish(jump, curvature, jumps_ref, curvature_ref):
    nrhs = jump.shape[0]
    faces = jump.shape[1] // 2
    half = nrhs // 2
    at_row, at_column = iota((nrhs, nrhs), 0), iota((nrhs, nrhs), 1)
    lay = unit(at_row == jnp.where(at_column < half, 2 * at_column, 2 * (at_column - half) + 1))
    for h in range(2):
        part = slice(h * half, (h + 1) * half)
        apart = jnp.concatenate([jump[part, :faces], jump[part, faces:]], axis=0)
        jumps_ref[part] = dot(lay, apart).astype(BF16).reshape(half, 2, faces)
    curvature_ref[...] = curvature[...]


def shards(multipliers, partner, interface_rows, block_mask, tiles, basis, coarse_inverse):
    nx = lax.axis_size("gx")
    ny = lax.axis_size("gy")
    lam = multipliers[0, 0]
    nrhs, _, faces = lam.shape
    rows = interface_rows[0]
    width = tiles.shape[2]
    nblock = block_mask.shape[2]
    four_cd = basis.shape[2]
    total = coarse_inverse.shape[1]
    row_cd = total // nx
    dma = pltpu.SemaphoreType.DMA
    vmem = pltpu.VMEM
    two = 2 * faces
    jump, curvature = pl.pallas_call(
        functools.partial(kernel, nx, ny),
        out_shape=(
            jax.ShapeDtypeStruct((nrhs, two), BF16),
            jax.ShapeDtypeStruct((1, nrhs), F32),
        ),
        in_specs=[pl.BlockSpec(memory_space=pl.ANY)] * 7,
        out_specs=(pl.BlockSpec(memory_space=vmem), pl.BlockSpec(memory_space=vmem)),
        scratch_shapes=[
            vmem(lam.shape, BF16),
            vmem((2, faces), I32),
            vmem(rows.shape, I32),
            vmem((nblock, nblock), I32),
            vmem((width, width), BF16),
            vmem((2 * four_cd, width), BF16),
            vmem((2 * row_cd, total), BF16),
            vmem((nrhs, two), BF16),
            vmem((nrhs, two), BF16),
            vmem((2, faces), I32),
            vmem((2, faces), I32),
            vmem((1, 2 * two), I32),
            vmem((nrhs, width), BF16),
            vmem((nrhs, 128), F32),
            vmem((nrhs + four_cd, width), BF16),
            vmem((nblock, 16, width), BF16),
            vmem((2 * nx * four_cd, ny * four_cd), BF16),
            vmem((ny * four_cd, nrhs), BF16),
            vmem((nx * four_cd, nrhs), BF16),
            vmem((2 * four_cd, two), BF16),
            vmem((four_cd, two), BF16),
            vmem((2 * nx * four_cd, nrhs), BF16),
            vmem((nx, 2 * four_cd, nrhs), BF16),
            vmem((nrhs, two), BF16),
            vmem((nrhs, two), BF16),
            vmem((nrhs, two), BF16),
            vmem((nx, 1, nrhs), F32),
            vmem((ny, 1, nrhs), F32),
            dma((13,)),
            dma((11,)),
            dma((11,)),
            dma((ny,)),
            dma((ny,)),
            dma((nx,)),
            dma((nx,)),
            dma((nx,)),
            dma((nx,)),
            dma((nx,)),
            dma((nx,)),
            dma((ny,)),
            dma((ny,)),
        ],
        compiler_params=pltpu.CompilerParams(
            collective_id=0, has_side_effects=True, vmem_limit_bytes=60 * 2**20
        ),
    )(lam, partner[0, 0], rows, block_mask[0, 0], tiles[0, 0], basis[0, 0], coarse_inverse)
    jumps, curvature = pl.pallas_call(
        finish,
        out_shape=(jax.ShapeDtypeStruct(lam.shape, BF16), jax.ShapeDtypeStruct((1, nrhs), F32)),
        in_specs=[pl.BlockSpec(memory_space=vmem)] * 2,
        out_specs=(pl.BlockSpec(memory_space=vmem), pl.BlockSpec(memory_space=vmem)),
    )(jump, curvature)
    return jumps[None, None], curvature.reshape(nrhs)


def solution(mesh):
    in_specs = (
        P("gx", "gy", None, None, None),
        P("gx", "gy", None, None),
        P("gx", "gy", None),
        P("gx", "gy", None, None),
        P("gx", "gy", None, None),
        P("gx", "gy", None, None),
        P(),
    )
    out_specs = (P("gx", "gy", None, None, None), P())
    return jax.shard_map(shards, mesh=mesh, in_specs=in_specs, out_specs=out_specs, check_vma=False)
```
